32 devices in a mesh: store: 8 (over y, x, core), tp: 4 (over z).
Axes of the slice: x: 2, y: 2, z: 4, core: 2. Of those that a mesh axis runs over, the one named last changes fastest.
Arguments:
- stored_hidden: bfloat16 [64, 128, 8192], P('store'), may hold values from -6 to 6
- kv_weight: bfloat16 [8192, 2, 1024], P(None, None, 'tp'), may hold values from -0.0625 to 0.0625
- new_query: bfloat16 [4096, 32, 128], P('store', 'tp'), may hold values from -176.7767 to 176.7767
- new_entries: bfloat16 [4096, 2, 8, 128], P('store', None, 'tp'), may hold values from -6.1 to 6.1
- out_weight: bfloat16 [4096, 4096], P('tp'), may hold values from -1.25 to 1.25
- prefix_len: int32 [16], replicated, may hold values from 257 to 512
- stretch_len: int32 [16], replicated, may hold values from 128 to 256
- block_loc: int32 [16, 4], replicated, may hold values from 0 to 63, as said below
- owner: int32 [16], replicated, may hold values from 0 to 15, as said below
Outputs:
- output: bfloat16 [4096, 4096], P('store', 'tp')
The draws below stay inside these ranges and needn't reach their ends.
Inputs may be any that keep to these rules, and one draw needn't show every extreme that they name: `owner`: a permutation; serving slot g lies on store index g // 2. `block_loc`: every stored block is named once; the blocks of the requests served on one store index lie on distinct store indices, stored block b on store index b // 8; blocks from ceil(prefix_len / 128) on are not read.
All inputs are finite; a program needn't handle non-finite values.
Results may differ from the reference program's by a relative error of at most 0.012.
Values may be sent and summed in bfloat16 or wider, within the bound.
A program may use at most 192 MiB of HBM per device.

```python
import jax
import jax.numpy as jnp
from jax import lax

D = 8192
D_OUT = 4096
KVH = 8
HD = 128
QH = 32
CH = 256
REQ_DEV = 2
PB = 4
BLK = 128
REQS = 16
NEW_TOTAL = 4096
STORE_BLOCKS = 64
N_STORE = 8
N_TP = 4


def layout(key):
    key_owner, key_sigma, key_offset, key_rho, key_tau = jax.random.split(key, 5)
    per_store = REQ_DEV * PB
    owner = jax.random.permutation(key_owner, REQS).astype(jnp.int32)
    sigma = jax.random.permutation(key_sigma, N_STORE).astype(jnp.int32)
    offsets = jax.random.permutation(key_offset, N_STORE)[:per_store].astype(jnp.int32)
    rho = jax.vmap(lambda subkey: jax.random.permutation(subkey, per_store))(jax.random.split(key_rho, N_STORE)).astype(jnp.int32)
    tau = jax.vmap(lambda subkey: jax.random.permutation(subkey, per_store))(jax.random.split(key_tau, N_STORE)).astype(jnp.int32)
    own_store = owner // REQ_DEV
    local_slot = owner % REQ_DEV
    order = rho[own_store[:, None], local_slot[:, None] * PB + jnp.arange(PB, dtype=jnp.int32)[None, :]]
    holder = sigma[(own_store[:, None] + offsets[order]) % N_STORE]
    place = tau[holder, order]
    return (owner, (holder * per_store + place).astype(jnp.int32))


def draw_owner(key, part):
    return layout(key)[0]


def draw_block_loc(key, part):
    return layout(key)[1]


def draw_prefix_len(key, part):
    key = jax.random.fold_in(key, 11)
    key_len, key_pick = jax.random.split(key)
    values = jax.random.randint(key_len, (REQS,), PB * BLK // 2 + 1, PB * BLK + 1)
    chosen = jax.random.randint(key_pick, (), 0, REQS)
    return jnp.where(jnp.arange(REQS) == chosen, PB * BLK, values).astype(jnp.int32)


def draw_stretch_len(key, part):
    key = jax.random.fold_in(key, 13)
    key_len, key_pick = jax.random.split(key)
    values = jax.random.randint(key_len, (REQS,), CH // 2, CH + 1)
    chosen = jax.random.randint(key_pick, (), 0, REQS)
    return jnp.where(jnp.arange(REQS) == chosen, CH, values).astype(jnp.int32)


def entry_base(key):
    return jax.random.truncated_normal(jax.random.fold_in(key, 101), -6.0, 6.0, (NEW_TOTAL, 2, KVH, HD), jnp.float32)


def draw_new_entries(key, part):
    base = entry_base(key)
    return base.astype(jnp.bfloat16)


def draw_new_query(key, part):
    key = jax.random.fold_in(key, 7)
    queries = 2.0 * jax.random.truncated_normal(key, -6.0, 6.0, (NEW_TOTAL, QH, HD), jnp.float32)
    return queries.astype(jnp.bfloat16)


def block_levels(key, shape, pieces, smallest, largest):
    def one(position, shards_of):
        draws = jax.random.uniform(jax.random.fold_in(jax.random.fold_in(key, 6), position), (shards_of,), jnp.float32, smallest / len(pieces), largest / len(pieces))
        return jnp.repeat(jnp.exp(draws), shape[position] // shards_of).reshape((-1,) + (1,) * (len(shape) - position - 1))

    level = one(*pieces[0])
    for cut in pieces[1:]:
        level = level * one(*cut)
    return level


def gaussian(own_key, dims, deviation, bound, cuts=(), kind=jnp.bfloat16):
    values = jax.random.normal(own_key, dims, jnp.float32) * deviation
    if len(cuts) > 0:
        values = block_levels(own_key, dims, cuts, -0.22, 0.18) * values
    return jnp.clip(values, min=-bound, max=bound).astype(kind)


def setup_inputs(seed: int = 0) -> dict:
    splits = jax.random.split(jax.random.key(seed), 10)
    return {
        "stored_hidden": gaussian(splits[0], (STORE_BLOCKS, BLK, D), 1.0, 6.0, ((0, 8),)),
        "kv_weight": gaussian(splits[1], (D, 2, KVH * HD), D ** -0.5, 0.0625, ((2, 4),)),
        "new_query": draw_new_query(jax.random.fold_in(splits[9], 71), 0),
        "new_entries": draw_new_entries(jax.random.fold_in(splits[9], 71), 0),
        "out_weight": gaussian(splits[4], (QH * HD, D_OUT), (5.0 / (QH * HD) ** 0.5), 1.25, ((0, 4),)),
        "prefix_len": draw_prefix_len(jax.random.fold_in(splits[9], 71), 0),
        "stretch_len": draw_stretch_len(jax.random.fold_in(splits[9], 71), 0),
        "block_loc": draw_block_loc(jax.random.fold_in(splits[9], 71), 0),
        "owner": draw_owner(jax.random.fold_in(splits[9], 71), 0),
    }


rope_base = 500000.0
mask_fill = -1.0e30


def rotary(values, count):
    head = values.shape[-1]
    half = head // 2
    positions = jnp.arange(count, dtype=jnp.float32)
    inverse = rope_base ** (-(jnp.arange(half, dtype=jnp.float32) * 2.0 / head))
    angles = positions[:, None] * inverse[None, :]
    cosine = jnp.cos(angles)[:, None, :]
    sine = jnp.sin(angles)[:, None, :]
    first = values[..., :half]
    second = values[..., half:]
    return jnp.concatenate([first * cosine - second * sine, second * cosine + first * sine], axis=-1)


def reference(stored_hidden, kv_weight, new_query, new_entries, out_weight, prefix_len, stretch_len, block_loc, owner):
    request_of = jnp.zeros((REQS,), jnp.int32).at[owner].set(jnp.arange(REQS, dtype=jnp.int32))
    projection = kv_weight.reshape(D, 2 * KVH * HD)
    out_wide = out_weight.astype(jnp.float32).reshape(N_TP, (QH // N_TP) * HD, D_OUT)
    span = PB * BLK
    scale = HD ** -0.5

    def serve(slot):
        request = request_of[slot]
        prefix_rows = stored_hidden[block_loc[request]].reshape(span, D)
        projected = jnp.dot(prefix_rows, projection, preferred_element_type=jnp.float32).reshape(span, 2, KVH, HD)
        keys = rotary(projected[:, 0], span).astype(jnp.bfloat16)
        values = projected[:, 1].astype(jnp.bfloat16)
        queries = lax.dynamic_slice_in_dim(new_query, slot * CH, CH, 0).astype(jnp.float32).reshape(CH, KVH, QH // KVH, HD)
        entries = lax.dynamic_slice_in_dim(new_entries, slot * CH, CH, 0).astype(jnp.float32)
        early = jnp.einsum('qkgd,pkd->kgqp', queries, keys.astype(jnp.float32)) * scale
        prefix_live = jnp.arange(span)[None, None, None, :] < prefix_len[request]
        early = jnp.where(prefix_live, early, mask_fill)
        recent = jnp.einsum('qkgd,jkd->kgqj', queries, entries[:, 0]) * scale
        causal = jnp.arange(CH)[None, :] <= jnp.arange(CH)[:, None]
        recent = jnp.where(causal[None, None], recent, mask_fill)
        top = jnp.maximum(early.max(-1), recent.max(-1))[..., None]
        early_w = jnp.exp(early - top)
        recent_w = jnp.exp(recent - top)
        total = early_w.sum(-1, keepdims=True) + recent_w.sum(-1, keepdims=True)
        early_p = lax.optimization_barrier((early_w / total).astype(jnp.bfloat16)).astype(jnp.float32)
        recent_p = lax.optimization_barrier((recent_w / total).astype(jnp.bfloat16)).astype(jnp.float32)
        attended = jnp.einsum('kgqp,pkd->qkgd', early_p, values.astype(jnp.float32))
        attended = attended + jnp.einsum('kgqj,jkd->qkgd', recent_p, entries[:, 1])
        attended = lax.optimization_barrier(attended.astype(jnp.bfloat16)).astype(jnp.float32)
        attended = attended.reshape(CH, N_TP, (QH // N_TP) * HD)
        partials = jnp.einsum('qtc,tcd->tqd', attended, out_wide)
        partials = lax.optimization_barrier(partials.astype(jnp.bfloat16)).astype(jnp.float32)
        summed = partials.sum(0)
        live = jnp.arange(CH) < stretch_len[request]
        return jnp.where(live[:, None], summed, 0.0).astype(jnp.bfloat16)

    return lax.map(serve, jnp.arange(REQS, dtype=jnp.int32)).reshape(REQS * CH, D_OUT)
```

```python
import jax
import jax.numpy as jnp
from jax import lax
from jax.sharding import PartitionSpec as P

rope_base = 500000.0
mask_fill = -1e30


def rotary_at(values, positions):
    head = values.shape[-1]
    half = head // 2
    inverse = rope_base ** (-(jnp.arange(half, dtype=jnp.float32) * 2.0 / head))
    angles = positions.astype(jnp.float32)[..., None] * inverse
    cosine = jnp.cos(angles)[..., None, :]
    sine = jnp.sin(angles)[..., None, :]
    first = values[..., :half]
    second = values[..., half:]
    return jnp.concatenate(
        [first * cosine - second * sine, second * cosine + first * sine], axis=-1
    )


def shards(
    stored_hidden,
    kv_weight,
    new_query,
    new_entries,
    out_weight,
    prefix_len,
    stretch_len,
    block_loc,
    owner,
):
    stores = lax.axis_size("store")
    own_store = lax.axis_index("store")
    local_blocks, block_rows, width = stored_hidden.shape
    request_count = owner.shape[0]
    per_owner = request_count // stores
    span_count = block_loc.shape[1]
    span = span_count * block_rows
    head = new_query.shape[2]
    query_heads = new_query.shape[1]
    kv_local = kv_weight.shape[2] // head
    group = query_heads // kv_local
    stretch = new_query.shape[0] // per_owner
    slot_ids = jnp.arange(request_count, dtype=jnp.int32)
    matched = owner[None, :] == slot_ids[:, None]
    request_of = jnp.sum(jnp.where(matched, slot_ids[None, :], 0), axis=1)
    locations = block_loc.reshape(-1)
    my_slots = own_store * per_owner + jnp.arange(per_owner, dtype=jnp.int32)
    my_requests = request_of[my_slots]
    senders = (block_loc[my_requests] // local_blocks).reshape(-1)
    local_ids = own_store * local_blocks + jnp.arange(local_blocks, dtype=jnp.int32)
    entry_ids = jnp.arange(locations.shape[0], dtype=jnp.int32)
    named = jnp.sum(
        jnp.where(locations[None, :] == local_ids[:, None], entry_ids[None, :], 0), axis=1
    )
    target = owner[named // span_count] // per_owner
    positions = (named % span_count)[:, None] * block_rows + jnp.arange(
        block_rows, dtype=jnp.int32
    )
    hidden = stored_hidden.reshape(-1, width)
    key_part = jnp.dot(hidden, kv_weight[:, 0], preferred_element_type=jnp.float32)
    value_part = jnp.dot(hidden, kv_weight[:, 1], preferred_element_type=jnp.float32)
    key_part = key_part.reshape(local_blocks, block_rows, kv_local, head)
    key_part = rotary_at(key_part, positions).astype(jnp.bfloat16)
    value_part = value_part.reshape(local_blocks, block_rows, kv_local, head).astype(jnp.bfloat16)
    both = jnp.stack([key_part, value_part], axis=1)
    slot = jnp.sum(
        jnp.where(
            target[None, :] == jnp.arange(stores, dtype=jnp.int32)[:, None],
            jnp.arange(local_blocks, dtype=jnp.int32)[None, :],
            0,
        ),
        axis=1,
    )
    incoming = lax.all_to_all(both[slot], "store", split_axis=0, concat_axis=0, tiled=True)
    fetched = incoming[senders].reshape(per_owner, span_count, 2, block_rows, kv_local, head)
    keys = fetched[:, :, 0].reshape(per_owner, span, kv_local, head)
    values = fetched[:, :, 1].reshape(per_owner, span, kv_local, head)
    queries = new_query.reshape(per_owner, stretch, kv_local, group, head)
    entries = new_entries.reshape(per_owner, stretch, 2, kv_local, head)
    scale = head ** (-0.5)
    early = (
        jnp.einsum("rqkgd,rpkd->rkgqp", queries, keys, preferred_element_type=jnp.float32) * scale
    )
    prefix_live = jnp.arange(span)[None, :] < prefix_len[my_requests][:, None]
    early = jnp.where(prefix_live[:, None, None, None, :], early, mask_fill)
    recent = (
        jnp.einsum(
            "rqkgd,rjkd->rkgqj", queries, entries[:, :, 0], preferred_element_type=jnp.float32
        )
        * scale
    )
    causal = jnp.arange(stretch)[None, :] <= jnp.arange(stretch)[:, None]
    recent = jnp.where(causal[None, None, None], recent, mask_fill)
    top = jnp.maximum(early.max(-1), recent.max(-1))[..., None]
    early_w = jnp.exp(early - top)
    recent_w = jnp.exp(recent - top)
    total = early_w.sum(-1, keepdims=True) + recent_w.sum(-1, keepdims=True)
    early_p = (early_w / total).astype(jnp.bfloat16)
    recent_p = (recent_w / total).astype(jnp.bfloat16)
    attended = jnp.einsum("rkgqp,rpkd->rqkgd", early_p, values, preferred_element_type=jnp.float32)
    attended = attended + jnp.einsum(
        "rkgqj,rjkd->rqkgd", recent_p, entries[:, :, 1], preferred_element_type=jnp.float32
    )
    attended = attended.astype(jnp.bfloat16).reshape(per_owner * stretch, query_heads * head)
    partial_value = (
        jnp.dot(attended, out_weight, preferred_element_type=jnp.float32)
        .astype(jnp.bfloat16)
        .astype(jnp.float32)
    )
    summed = lax.psum_scatter(
        partial_value.astype(jnp.bfloat16), "tp", scatter_dimension=1, tiled=True
    ).astype(jnp.float32)
    live = (jnp.arange(stretch)[None, :] < stretch_len[my_requests][:, None]).reshape(-1)
    return jnp.where(live[:, None], summed, 0.0).astype(jnp.bfloat16)


def solution(mesh):
    in_specs = (
        P("store", None, None),
        P(None, None, "tp"),
        P("store", "tp", None),
        P("store", None, "tp", None),
        P("tp", None),
        P(),
        P(),
        P(),
        P(),
    )
    out_specs = P("store", "tp")
    return jax.shard_map(shards, mesh=mesh, in_specs=in_specs, out_specs=out_specs, check_vma=False)
```

```python
import functools

import jax
import jax.numpy as jnp
from jax import lax
from jax.experimental import pallas as pl
from jax.experimental.pallas import tpu as pltpu
from jax.sharding import PartitionSpec as P

rope_base = 500000.0
mask_fill = -1e30


def rotary_at(values, positions):
    head = values.shape[-1]
    half = head // 2
    inverse = rope_base ** (-(jnp.arange(half, dtype=jnp.float32) * 2.0 / head))
    angles = positions.astype(jnp.float32)[..., None] * inverse
    cosine = jnp.cos(angles)[..., None, :]
    sine = jnp.sin(angles)[..., None, :]
    first = values[..., :half]
    second = values[..., half:]
    return jnp.concatenate(
        [first * cosine - second * sine, second * cosine + first * sine], axis=-1
    )


def reduce_kernel(
    groups,
    pieces,
    rows_ref,
    weight_ref,
    out_ref,
    weight_buf,
    part,
    total,
    from_left,
    from_right,
    weight_sem,
    right_send,
    right_recv,
    left_send,
    left_recv,
):
    me = lax.axis_index("tp")
    wide = weight_buf.shape[3]
    last = groups - 1
    upper = jnp.where(me < groups // 2, 1, 0)

    def group_at(step):
        return upper * (last - step) + (1 - upper) * step

    def weight_copy(group, piece):
        start = pl.multiple_of((group * pieces + piece) * wide, wide)
        return pltpu.make_async_copy(
            weight_ref.at[:, pl.ds(start, wide)],
            weight_buf.at[group, piece],
            weight_sem.at[group, piece],
        )

    def right_copy(group, piece):
        return pltpu.make_async_remote_copy(
            src_ref=part.at[group, piece],
            dst_ref=from_left.at[group, piece],
            send_sem=right_send.at[group, piece],
            recv_sem=right_recv.at[group, piece],
            device_id={"tp": me + 1},
            device_id_type=pl.DeviceIdType.MESH,
        )

    def left_copy(group, piece):
        return pltpu.make_async_remote_copy(
            src_ref=part.at[group, piece],
            dst_ref=from_right.at[group, piece],
            send_sem=left_send.at[group, piece],
            recv_sem=left_recv.at[group, piece],
            device_id={"tp": me - 1},
            device_id_type=pl.DeviceIdType.MESH,
        )

    def each(body):
        def step(index, carry):
            body(index // pieces, index % pieces)
            return carry

        lax.fori_loop(0, groups * pieces, step, 0)

    each(lambda step, piece: weight_copy(group_at(step), piece).start())

    barrier = pltpu.get_barrier_semaphore()

    @pl.when(me > 0)
    def _():
        pl.semaphore_signal(
            barrier, inc=1, device_id={"tp": me - 1}, device_id_type=pl.DeviceIdType.MESH
        )

    @pl.when(me < last)
    def _():
        pl.semaphore_signal(
            barrier, inc=1, device_id={"tp": me + 1}, device_id_type=pl.DeviceIdType.MESH
        )

    pl.semaphore_wait(barrier, jnp.where(me > 0, 1, 0) + jnp.where(me < last, 1, 0))

    def produce(step, piece):
        group = group_at(step)
        weight_copy(group, piece).wait()
        product = jnp.dot(
            rows_ref[...], weight_buf[group, piece], preferred_element_type=jnp.float32
        ).astype(part.dtype)
        part[group, piece] = product

        @pl.when(group == me)
        def _():
            total[piece] = product.astype(jnp.float32)

        @pl.when((me == 0) & (group > me))
        def _():
            right_copy(group, piece).start()

        @pl.when((me == last) & (group < me))
        def _():
            left_copy(group, piece).start()

    each(produce)

    def add(group, piece, arrived):
        summed = part[group, piece].astype(jnp.float32) + arrived[group, piece].astype(jnp.float32)
        part[group, piece] = summed.astype(part.dtype)

    def pass_on(step, piece):
        right = last - step

        @pl.when((me > 0) & (right >= me))
        def _():
            right_copy(right, piece).wait_recv()

        @pl.when((me > 0) & (right > me))
        def _():
            add(right, piece, from_left)
            right_copy(right, piece).start()

        @pl.when((me > 0) & (right == me))
        def _():
            total[piece] += from_left[right, piece].astype(jnp.float32)

        left = step

        @pl.when((me < last) & (left <= me))
        def _():
            left_copy(left, piece).wait_recv()

        @pl.when((me < last) & (left < me))
        def _():
            add(left, piece, from_right)
            left_copy(left, piece).start()

        @pl.when((me < last) & (left == me))
        def _():
            total[piece] += from_right[left, piece].astype(jnp.float32)

    each(pass_on)

    for piece in range(pieces):
        out_ref[:, piece * wide : (piece + 1) * wide] = total[piece].astype(out_ref.dtype)

    def settle(group, piece):
        @pl.when(group > me)
        def _():
            right_copy(group, piece).wait_send()

        @pl.when(group < me)
        def _():
            left_copy(group, piece).wait_send()

    each(settle)


def projected_sum(rows, weight, groups):
    count, depth = rows.shape
    columns = weight.shape[1] // groups
    pieces = 2
    wide = columns // pieces
    slots = (groups, pieces, count, wide)
    return pl.pallas_call(
        functools.partial(reduce_kernel, groups, pieces),
        out_shape=jax.ShapeDtypeStruct((count, columns), jnp.bfloat16),
        in_specs=[
            pl.BlockSpec(memory_space=pltpu.VMEM),
            pl.BlockSpec(memory_space=pl.ANY),
        ],
        out_specs=pl.BlockSpec(memory_space=pltpu.VMEM),
        scratch_shapes=[
            pltpu.VMEM((groups, pieces, depth, wide), jnp.bfloat16),
            pltpu.VMEM(slots, jnp.bfloat16),
            pltpu.VMEM((pieces, count, wide), jnp.float32),
            pltpu.VMEM(slots, jnp.bfloat16),
            pltpu.VMEM(slots, jnp.bfloat16),
        ]
        + [pltpu.SemaphoreType.DMA((groups, pieces))] * 5,
        compiler_params=pltpu.CompilerParams(
            collective_id=0, has_side_effects=True, vmem_limit_bytes=44 * 1024 * 1024
        ),
        cost_estimate=pl.CostEstimate(
            flops=2 * count * depth * columns * groups,
            bytes_accessed=weight.size * 2,
            transcendentals=0,
        ),
        name="projected_sum",
    )(rows, weight)


def shards(
    stored_hidden,
    kv_weight,
    new_query,
    new_entries,
    out_weight,
    prefix_len,
    stretch_len,
    block_loc,
    owner,
):
    stores = lax.axis_size("store")
    own_store = lax.axis_index("store")
    local_blocks, block_rows, width = stored_hidden.shape
    request_count = owner.shape[0]
    per_owner = request_count // stores
    span_count = block_loc.shape[1]
    span = span_count * block_rows
    head = new_query.shape[2]
    query_heads = new_query.shape[1]
    kv_local = kv_weight.shape[2] // head
    group = query_heads // kv_local
    stretch = new_query.shape[0] // per_owner
    slot_ids = jnp.arange(request_count, dtype=jnp.int32)
    matched = owner[None, :] == slot_ids[:, None]
    request_of = jnp.sum(jnp.where(matched, slot_ids[None, :], 0), axis=1)
    locations = block_loc.reshape(-1)
    my_slots = own_store * per_owner + jnp.arange(per_owner, dtype=jnp.int32)
    my_requests = request_of[my_slots]
    senders = (block_loc[my_requests] // local_blocks).reshape(-1)
    local_ids = own_store * local_blocks + jnp.arange(local_blocks, dtype=jnp.int32)
    entry_ids = jnp.arange(locations.shape[0], dtype=jnp.int32)
    named = jnp.sum(
        jnp.where(locations[None, :] == local_ids[:, None], entry_ids[None, :], 0), axis=1
    )
    target = owner[named // span_count] // per_owner
    positions = (named % span_count)[:, None] * block_rows + jnp.arange(
        block_rows, dtype=jnp.int32
    )
    hidden = stored_hidden.reshape(-1, width)
    key_part = jnp.dot(hidden, kv_weight[:, 0], preferred_element_type=jnp.float32)
    value_part = jnp.dot(hidden, kv_weight[:, 1], preferred_element_type=jnp.float32)
    key_part = key_part.reshape(local_blocks, block_rows, kv_local, head)
    key_part = rotary_at(key_part, positions).astype(jnp.bfloat16)
    value_part = value_part.reshape(local_blocks, block_rows, kv_local, head).astype(jnp.bfloat16)
    both = jnp.stack([key_part, value_part], axis=1)
    slot = jnp.sum(
        jnp.where(
            target[None, :] == jnp.arange(stores, dtype=jnp.int32)[:, None],
            jnp.arange(local_blocks, dtype=jnp.int32)[None, :],
            0,
        ),
        axis=1,
    )
    incoming = lax.all_to_all(both[slot], "store", split_axis=0, concat_axis=0, tiled=True)
    fetched = incoming[senders].reshape(per_owner, span_count, 2, block_rows, kv_local, head)
    keys = fetched[:, :, 0].reshape(per_owner, span, kv_local, head)
    values = fetched[:, :, 1].reshape(per_owner, span, kv_local, head)
    queries = new_query.reshape(per_owner, stretch, kv_local, group, head)
    entries = new_entries.reshape(per_owner, stretch, 2, kv_local, head)
    scale = head ** (-0.5)
    early = (
        jnp.einsum("rqkgd,rpkd->rkgqp", queries, keys, preferred_element_type=jnp.float32) * scale
    )
    prefix_live = jnp.arange(span)[None, :] < prefix_len[my_requests][:, None]
    early = jnp.where(prefix_live[:, None, None, None, :], early, mask_fill)
    recent = (
        jnp.einsum(
            "rqkgd,rjkd->rkgqj", queries, entries[:, :, 0], preferred_element_type=jnp.float32
        )
        * scale
    )
    causal = jnp.arange(stretch)[None, :] <= jnp.arange(stretch)[:, None]
    recent = jnp.where(causal[None, None, None], recent, mask_fill)
    top = jnp.maximum(early.max(-1), recent.max(-1))[..., None]
    early_w = jnp.exp(early - top)
    recent_w = jnp.exp(recent - top)
    total = early_w.sum(-1, keepdims=True) + recent_w.sum(-1, keepdims=True)
    early_p = (early_w / total).astype(jnp.bfloat16)
    recent_p = (recent_w / total).astype(jnp.bfloat16)
    attended = jnp.einsum("rkgqp,rpkd->rqkgd", early_p, values, preferred_element_type=jnp.float32)
    attended = attended + jnp.einsum(
        "rkgqj,rjkd->rqkgd", recent_p, entries[:, :, 1], preferred_element_type=jnp.float32
    )
    attended = attended.astype(jnp.bfloat16).reshape(per_owner * stretch, query_heads * head)
    live = (jnp.arange(stretch)[None, :] < stretch_len[my_requests][:, None]).reshape(-1)
    attended = jnp.where(live[:, None], attended, jnp.zeros((), attended.dtype))
    return projected_sum(attended, out_weight, lax.axis_size("tp"))


def solution(mesh):
    in_specs = (
        P("store", None, None),
        P(None, None, "tp"),
        P("store", "tp", None),
        P("store", None, "tp", None),
        P("tp", None),
        P(),
        P(),
        P(),
        P(),
    )
    out_specs = P("store", "tp")
    return jax.shard_map(shards, mesh=mesh, in_specs=in_specs, out_specs=out_specs, check_vma=False)
```

```python
import functools

import jax
import jax.numpy as jnp
import numpy as np
from jax import lax
from jax.experimental import pallas as pl
from jax.experimental.pallas import tpu as pltpu
from jax.sharding import PartitionSpec as P

rope_base = 500000.0
mask_fill = -1e30


def rotary_table(span, head):
    half = head // 2
    exponents = -(np.arange(half, dtype=np.float32) * np.float32(2.0 / head))
    inverse = np.power(np.float32(rope_base), exponents)
    angles = np.arange(span, dtype=np.float32)[:, None] * inverse[None, :]
    cosine = np.cos(angles)
    sine = np.sin(angles)
    return (
        np.concatenate([cosine, cosine], axis=1),
        np.concatenate([-sine, sine], axis=1),
    )


def project_kernel(
    target_ref, place_ref, hidden_ref, weight_ref, cosine_ref, sine_ref, out_ref, key_sum, value_sum
):
    step = pl.program_id(0)
    head = cosine_ref.shape[2]
    wide = weight_ref.shape[2]
    blocks, block_rows, depth = hidden_ref.shape
    hidden = hidden_ref[...].reshape(blocks * block_rows, depth)
    w = jnp.swapaxes(weight_ref[...],0,1)
    key_part = jnp.dot(hidden, w[0], preferred_element_type=jnp.float32)
    value_part = jnp.dot(hidden, w[1], preferred_element_type=jnp.float32)

    @pl.when(step == 0)
    def _():
        key_sum[...] = key_part
        value_sum[...] = value_part

    @pl.when(step > 0)
    def _():
        key_sum[...] += key_part
        value_sum[...] += value_part

    @pl.when(step == pl.num_programs(0) - 1)
    def _():
        for block in range(blocks):
            rows = pl.ds(block * block_rows, block_rows)
            cosine = cosine_ref[place_ref[block]]
            sine = sine_ref[place_ref[block]]
            slot = target_ref[block]
            for start in range(0, wide, head):
                part = key_sum[rows, start : start + head]
                turned = part * cosine + pltpu.roll(part, head // 2, 1) * sine
                out_ref[slot, :, start : start + head] = turned.astype(out_ref.dtype)
            out_ref[slot, :, wide:] = value_sum[rows, :].astype(out_ref.dtype)


def project(target, place, hidden, weight, span_count, head, slots):
    blocks, block_rows, width = hidden.shape
    wide = weight.shape[2]
    depth = 1024
    cosine, sine = rotary_table(span_count * block_rows, head)
    table = (span_count, block_rows, head)
    whole = lambda shape: pl.BlockSpec(shape, lambda step, *_: (0,) * len(shape))
    return pl.pallas_call(
        project_kernel,
        out_shape=jax.ShapeDtypeStruct((slots, block_rows, 2 * wide), jnp.bfloat16),
        grid_spec=pltpu.PrefetchScalarGridSpec(
            num_scalar_prefetch=2,
            grid=(width // depth,),
            in_specs=[
                pl.BlockSpec((blocks, block_rows, depth), lambda step, *_: (0, 0, step)),
                pl.BlockSpec((depth, 2, wide), lambda step, *_: (step, 0, 0)),
                whole(table),
                whole(table),
            ],
            out_specs=whole((slots, block_rows, 2 * wide)),
            scratch_shapes=[pltpu.VMEM((blocks * block_rows, wide), jnp.float32)] * 2,
        ),
        compiler_params=pltpu.CompilerParams(vmem_limit_bytes=40 * 1024 * 1024),
        name="project",
    )(target, place, hidden, weight, cosine.reshape(table), sine.reshape(table))


def attend_kernel(
    sender_ref, prefix_ref, stretch_ref, query_ref, key_ref, value_ref, *block_refs_and_out
):
    block_refs, out_ref = block_refs_and_out[:-1], block_refs_and_out[-1]
    request = pl.program_id(0)
    heads, rows, head = query_ref.shape
    kv_heads = key_ref.shape[0]
    group = heads // kv_heads
    span = len(block_refs) * block_refs[0].shape[1]
    scale = head ** (-0.5)
    prefix_live = lax.broadcasted_iota(jnp.int32, (rows, span), 1) < prefix_ref[request]
    row_ids = lax.broadcasted_iota(jnp.int32, (rows, rows), 0)
    causal = lax.broadcasted_iota(jnp.int32, (rows, rows), 1) <= row_ids
    live = lax.broadcasted_iota(jnp.int32, (rows, head), 0) < stretch_ref[request]
    contract_last = (((1,), (1,)), ((), ()))
    for kv in range(kv_heads):
        lanes = slice(kv * head, (kv + 1) * head)
        value_lanes = slice((kv_heads + kv) * head, (kv_heads + kv + 1) * head)
        keys = jnp.concatenate([ref[0, :, lanes] for ref in block_refs], axis=0)
        values = jnp.concatenate([ref[0, :, value_lanes] for ref in block_refs], axis=0)
        new_keys = key_ref[kv]
        new_values = value_ref[kv]
        for index in range(group):
            h = kv * group + index
            query = query_ref[h]
            early = lax.dot_general(
                query, keys, contract_last, preferred_element_type=jnp.float32
            )
            recent = lax.dot_general(
                query, new_keys, contract_last, preferred_element_type=jnp.float32
            )
            early = jnp.where(prefix_live, early * scale, mask_fill)
            recent = jnp.where(causal, recent * scale, mask_fill)
            top = jnp.maximum(
                jnp.max(early, axis=1, keepdims=True), jnp.max(recent, axis=1, keepdims=True)
            )
            early_w = jnp.exp(early - top)
            recent_w = jnp.exp(recent - top)
            total = jnp.sum(early_w, axis=1, keepdims=True) + jnp.sum(
                recent_w, axis=1, keepdims=True
            )
            attended = jnp.dot(
                early_w.astype(jnp.bfloat16), values, preferred_element_type=jnp.float32
            ) + jnp.dot(
                recent_w.astype(jnp.bfloat16), new_values, preferred_element_type=jnp.float32
            )
            attended = jnp.where(live, attended / total, 0.0)
            out_ref[:, h * head : (h + 1) * head] = attended.astype(out_ref.dtype)


def attend(senders, prefix_len, stretch_len, query, keys, values, incoming):
    heads, count, head = query.shape
    kv_heads = keys.shape[0]
    requests = prefix_len.shape[0]
    rows = count // requests
    span_count = senders.shape[0] // requests
    _, block_rows, wide = incoming.shape

    def block_spec(j):
        return pl.BlockSpec(
            (1, block_rows, wide), lambda r, sender, *_: (sender[r * span_count + j], 0, 0)
        )

    return pl.pallas_call(
        attend_kernel,
        out_shape=jax.ShapeDtypeStruct((count, heads * head), jnp.bfloat16),
        grid_spec=pltpu.PrefetchScalarGridSpec(
            num_scalar_prefetch=3,
            grid=(requests,),
            in_specs=[
                pl.BlockSpec((heads, rows, head), lambda r, *_: (0, r, 0)),
                pl.BlockSpec((kv_heads, rows, head), lambda r, *_: (0, r, 0)),
                pl.BlockSpec((kv_heads, rows, head), lambda r, *_: (0, r, 0)),
            ]
            + [block_spec(j) for j in range(span_count)],
            out_specs=pl.BlockSpec((rows, heads * head), lambda r, *_: (r, 0)),
        ),
        compiler_params=pltpu.CompilerParams(vmem_limit_bytes=40 * 1024 * 1024),
        name="attend",
    )(senders, prefix_len, stretch_len, query, keys, values, *([incoming] * span_count))


def reduce_kernel(
    groups,
    pieces,
    rows_ref,
    weight_ref,
    out_ref,
    weight_buf,
    part,
    total,
    from_left,
    from_right,
    weight_sem,
    right_send,
    right_recv,
    left_send,
    left_recv,
):
    me = lax.axis_index("tp")
    wide = weight_buf.shape[3]
    last = groups - 1
    upper = jnp.where(me < groups // 2, 1, 0)

    def group_at(step):
        return upper * (last - step) + (1 - upper) * step

    def weight_copy(group, piece):
        start = pl.multiple_of((group * pieces + piece) * wide, wide)
        return pltpu.make_async_copy(
            weight_ref.at[:, pl.ds(start, wide)],
            weight_buf.at[group, piece],
            weight_sem.at[group, piece],
        )

    def right_copy(group, piece):
        return pltpu.make_async_remote_copy(
            src_ref=part.at[group, piece],
            dst_ref=from_left.at[group, piece],
            send_sem=right_send.at[group, piece],
            recv_sem=right_recv.at[group, piece],
            device_id={"tp": me + 1},
            device_id_type=pl.DeviceIdType.MESH,
        )

    def left_copy(group, piece):
        return pltpu.make_async_remote_copy(
            src_ref=part.at[group, piece],
            dst_ref=from_right.at[group, piece],
            send_sem=left_send.at[group, piece],
            recv_sem=left_recv.at[group, piece],
            device_id={"tp": me - 1},
            device_id_type=pl.DeviceIdType.MESH,
        )

    def each(body):
        def step(index, carry):
            body(index // pieces, index % pieces)
            return carry

        lax.fori_loop(0, groups * pieces, step, 0)

    each(lambda step, piece: weight_copy(group_at(step), piece).start())

    barrier = pltpu.get_barrier_semaphore()

    @pl.when(me > 0)
    def _():
        pl.semaphore_signal(
            barrier, inc=1, device_id={"tp": me - 1}, device_id_type=pl.DeviceIdType.MESH
        )

    @pl.when(me < last)
    def _():
        pl.semaphore_signal(
            barrier, inc=1, device_id={"tp": me + 1}, device_id_type=pl.DeviceIdType.MESH
        )

    pl.semaphore_wait(barrier, jnp.where(me > 0, 1, 0) + jnp.where(me < last, 1, 0))

    def produce(step, piece):
        group = group_at(step)
        weight_copy(group, piece).wait()
        product = jnp.dot(
            rows_ref[...], weight_buf[group, piece], preferred_element_type=jnp.float32
        ).astype(part.dtype)
        part[group, piece] = product

        @pl.when(group == me)
        def _():
            total[piece] = product.astype(jnp.float32)

        @pl.when((me == 0) & (group > me))
        def _():
            right_copy(group, piece).start()

        @pl.when((me == last) & (group < me))
        def _():
            left_copy(group, piece).start()

    each(produce)

    def add(group, piece, arrived):
        summed = part[group, piece].astype(jnp.float32) + arrived[group, piece].astype(jnp.float32)
        part[group, piece] = summed.astype(part.dtype)

    def pass_on(step, piece):
        right = last - step

        @pl.when((me > 0) & (right >= me))
        def _():
            right_copy(right, piece).wait_recv()

        @pl.when((me > 0) & (right > me))
        def _():
            add(right, piece, from_left)
            right_copy(right, piece).start()

        @pl.when((me > 0) & (right == me))
        def _():
            total[piece] += from_left[right, piece].astype(jnp.float32)

        left = step

        @pl.when((me < last) & (left <= me))
        def _():
            left_copy(left, piece).wait_recv()

        @pl.when((me < last) & (left < me))
        def _():
            add(left, piece, from_right)
            left_copy(left, piece).start()

        @pl.when((me < last) & (left == me))
        def _():
            total[piece] += from_right[left, piece].astype(jnp.float32)

    each(pass_on)

    for piece in range(pieces):
        out_ref[:, piece * wide : (piece + 1) * wide] = total[piece].astype(out_ref.dtype)

    def settle(group, piece):
        @pl.when(group > me)
        def _():
            right_copy(group, piece).wait_send()

        @pl.when(group < me)
        def _():
            left_copy(group, piece).wait_send()

    each(settle)


def projected_sum(rows, weight, groups):
    count, depth = rows.shape
    columns = weight.shape[1] // groups
    pieces = 2
    wide = columns // pieces
    slots = (groups, pieces, count, wide)
    return pl.pallas_call(
        functools.partial(reduce_kernel, groups, pieces),
        out_shape=jax.ShapeDtypeStruct((count, columns), jnp.bfloat16),
        in_specs=[
            pl.BlockSpec(memory_space=pltpu.VMEM),
            pl.BlockSpec(memory_space=pl.ANY),
        ],
        out_specs=pl.BlockSpec(memory_space=pltpu.VMEM),
        scratch_shapes=[
            pltpu.VMEM((groups, pieces, depth, wide), jnp.bfloat16),
            pltpu.VMEM(slots, jnp.bfloat16),
            pltpu.VMEM((pieces, count, wide), jnp.float32),
            pltpu.VMEM(slots, jnp.bfloat16),
            pltpu.VMEM(slots, jnp.bfloat16),
        ]
        + [pltpu.SemaphoreType.DMA((groups, pieces))] * 5,
        compiler_params=pltpu.CompilerParams(
            collective_id=0, has_side_effects=True, vmem_limit_bytes=44 * 1024 * 1024
        ),
        cost_estimate=pl.CostEstimate(
            flops=2 * count * depth * columns * groups,
            bytes_accessed=weight.size * 2,
            transcendentals=0,
        ),
        name="projected_sum",
    )(rows, weight)


def shards(
    stored_hidden,
    kv_weight,
    new_query,
    new_entries,
    out_weight,
    prefix_len,
    stretch_len,
    block_loc,
    owner,
):
    stores = lax.axis_size("store")
    own_store = lax.axis_index("store")
    local_blocks, block_rows, width = stored_hidden.shape
    request_count = owner.shape[0]
    per_owner = request_count // stores
    span_count = block_loc.shape[1]
    span = span_count * block_rows
    head = new_query.shape[2]
    query_heads = new_query.shape[1]
    kv_local = kv_weight.shape[2] // head
    group = query_heads // kv_local
    stretch = new_query.shape[0] // per_owner
    slot_ids = jnp.arange(request_count, dtype=jnp.int32)
    matched = owner[None, :] == slot_ids[:, None]
    request_of = jnp.sum(jnp.where(matched, slot_ids[None, :], 0), axis=1)
    locations = block_loc.reshape(-1)
    my_slots = own_store * per_owner + jnp.arange(per_owner, dtype=jnp.int32)
    my_requests = request_of[my_slots]
    senders = (block_loc[my_requests] // local_blocks).reshape(-1)
    local_ids = own_store * local_blocks + jnp.arange(local_blocks, dtype=jnp.int32)
    entry_ids = jnp.arange(locations.shape[0], dtype=jnp.int32)
    named = jnp.sum(
        jnp.where(locations[None, :] == local_ids[:, None], entry_ids[None, :], 0), axis=1
    )
    target = owner[named // span_count] // per_owner
    sent = project(
        target, named % span_count, stored_hidden, kv_weight, span_count, head, stores
    )
    incoming = lax.all_to_all(sent, "store", split_axis=0, concat_axis=0, tiled=True)
    attended = attend(
        senders,
        prefix_len[my_requests],
        stretch_len[my_requests],
        jnp.transpose(new_query, (1, 0, 2)),
        jnp.transpose(new_entries[:, 0], (1, 0, 2)),
        jnp.transpose(new_entries[:, 1], (1, 0, 2)),
        incoming,
    )
    return projected_sum(attended, out_weight, lax.axis_size("tp"))


def solution(mesh):
    in_specs = (
        P("store", None, None),
        P(None, None, "tp"),
        P("store", "tp", None),
        P("store", None, "tp", None),
        P("tp", None),
        P(),
        P(),
        P(),
        P(),
    )
    out_specs = P("store", "tp")
    return jax.shard_map(shards, mesh=mesh, in_specs=in_specs, out_specs=out_specs, check_vma=False)
```

```python
import functools

import jax
import jax.numpy as jnp
import numpy as np
from jax import lax
from jax.experimental import pallas as pl
from jax.experimental.pallas import tpu as pltpu
from jax.sharding import PartitionSpec as P

rope_base = 500000.0
mask_fill = -1e30


def rotary_table(span, head):
    half = head // 2
    exponents = -(np.arange(half, dtype=np.float32) * np.float32(2.0 / head))
    inverse = np.power(np.float32(rope_base), exponents)
    angles = np.arange(span, dtype=np.float32)[:, None] * inverse[None, :]
    cosine = np.cos(angles)
    sine = np.sin(angles)
    return (
        np.concatenate([cosine, cosine], axis=1),
        np.concatenate([-sine, sine], axis=1),
    )


def project_kernel(
    target_ref, place_ref, hidden_ref, weight_ref, cosine_ref, sine_ref, out_ref, key_sum, value_sum
):
    step = pl.program_id(0)
    head = cosine_ref.shape[2]
    wide = weight_ref.shape[2]
    blocks, block_rows, depth = hidden_ref.shape
    hidden = hidden_ref[...].reshape(blocks * block_rows, depth)
    w = jnp.swapaxes(weight_ref[...],0,1)
    key_part = jnp.dot(hidden, w[0], preferred_element_type=jnp.float32)
    value_part = jnp.dot(hidden, w[1], preferred_element_type=jnp.float32)

    @pl.when(step == 0)
    def _():
        key_sum[...] = key_part
        value_sum[...] = value_part

    @pl.when(step > 0)
    def _():
        key_sum[...] += key_part
        value_sum[...] += value_part

    @pl.when(step == pl.num_programs(0) - 1)
    def _():
        for block in range(blocks):
            rows = pl.ds(block * block_rows, block_rows)
            cosine = cosine_ref[place_ref[block]]
            sine = sine_ref[place_ref[block]]
            slot = target_ref[block]
            for start in range(0, wide, head):
                part = key_sum[rows, start : start + head]
                turned = part * cosine + pltpu.roll(part, head // 2, 1) * sine
                out_ref[slot, :, start : start + head] = turned.astype(out_ref.dtype)
            out_ref[slot, :, wide:] = value_sum[rows, :].astype(out_ref.dtype)


def project(target, place, hidden, weight, span_count, head, slots):
    blocks, block_rows, width = hidden.shape
    wide = weight.shape[2]
    depth = 1024
    cosine, sine = rotary_table(span_count * block_rows, head)
    table = (span_count, block_rows, head)
    whole = lambda shape: pl.BlockSpec(shape, lambda step, *_: (0,) * len(shape))
    return pl.pallas_call(
        project_kernel,
        out_shape=jax.ShapeDtypeStruct((slots, block_rows, 2 * wide), jnp.bfloat16),
        grid_spec=pltpu.PrefetchScalarGridSpec(
            num_scalar_prefetch=2,
            grid=(width // depth,),
            in_specs=[
                pl.BlockSpec((blocks, block_rows, depth), lambda step, *_: (0, 0, step)),
                pl.BlockSpec((depth, 2, wide), lambda step, *_: (step, 0, 0)),
                whole(table),
                whole(table),
            ],
            out_specs=whole((slots, block_rows, 2 * wide)),
            scratch_shapes=[pltpu.VMEM((blocks * block_rows, wide), jnp.float32)] * 2,
        ),
        compiler_params=pltpu.CompilerParams(vmem_limit_bytes=60 * 1024 * 1024),
        name="project",
    )(target, place, hidden, weight, cosine.reshape(table), sine.reshape(table))


def attend_kernel(
    sender_ref, prefix_ref, stretch_ref, query_ref, key_ref, value_ref, *block_refs_and_out
):
    block_refs, out_ref = block_refs_and_out[:-1], block_refs_and_out[-1]
    request = pl.program_id(0)
    heads, rows, head = query_ref.shape
    kv_heads = key_ref.shape[0]
    group = heads // kv_heads
    span = len(block_refs) * block_refs[0].shape[1]
    scale = head ** (-0.5)
    prefix_live = lax.broadcasted_iota(jnp.int32, (rows, span), 1) < prefix_ref[request]
    row_ids = lax.broadcasted_iota(jnp.int32, (rows, rows), 0)
    causal = lax.broadcasted_iota(jnp.int32, (rows, rows), 1) <= row_ids
    live = lax.broadcasted_iota(jnp.int32, (rows, head), 0) < stretch_ref[request]
    contract_last = (((1,), (1,)), ((), ()))
    for kv in range(kv_heads):
        lanes = slice(kv * head, (kv + 1) * head)
        value_lanes = slice((kv_heads + kv) * head, (kv_heads + kv + 1) * head)
        keys = jnp.concatenate([ref[0, :, lanes] for ref in block_refs], axis=0)
        values = jnp.concatenate([ref[0, :, value_lanes] for ref in block_refs], axis=0)
        new_keys = key_ref[kv]
        new_values = value_ref[kv]
        for index in range(group):
            h = kv * group + index
            query = query_ref[h]
            early = lax.dot_general(
                query, keys, contract_last, preferred_element_type=jnp.float32
            )
            recent = lax.dot_general(
                query, new_keys, contract_last, preferred_element_type=jnp.float32
            )
            early = jnp.where(prefix_live, early * scale, mask_fill)
            recent = jnp.where(causal, recent * scale, mask_fill)
            top = jnp.maximum(
                jnp.max(early, axis=1, keepdims=True), jnp.max(recent, axis=1, keepdims=True)
            )
            early_w = jnp.exp(early - top)
            recent_w = jnp.exp(recent - top)
            total = jnp.sum(early_w, axis=1, keepdims=True) + jnp.sum(
                recent_w, axis=1, keepdims=True
            )
            attended = jnp.dot(
                early_w.astype(jnp.bfloat16), values, preferred_element_type=jnp.float32
            ) + jnp.dot(
                recent_w.astype(jnp.bfloat16), new_values, preferred_element_type=jnp.float32
            )
            attended = jnp.where(live, attended / total, 0.0)
            out_ref[:, h * head : (h + 1) * head] = attended.astype(out_ref.dtype)


def attend(senders, prefix_len, stretch_len, query, keys, values, incoming):
    heads, count, head = query.shape
    kv_heads = keys.shape[0]
    requests = prefix_len.shape[0]
    rows = count // requests
    span_count = senders.shape[0] // requests
    _, block_rows, wide = incoming.shape

    def block_spec(j):
        return pl.BlockSpec(
            (1, block_rows, wide), lambda r, sender, *_: (sender[r * span_count + j], 0, 0)
        )

    return pl.pallas_call(
        attend_kernel,
        out_shape=jax.ShapeDtypeStruct((count, heads * head), jnp.bfloat16),
        grid_spec=pltpu.PrefetchScalarGridSpec(
            num_scalar_prefetch=3,
            grid=(requests,),
            in_specs=[
                pl.BlockSpec((heads, rows, head), lambda r, *_: (0, r, 0)),
                pl.BlockSpec((kv_heads, rows, head), lambda r, *_: (0, r, 0)),
                pl.BlockSpec((kv_heads, rows, head), lambda r, *_: (0, r, 0)),
            ]
            + [block_spec(j) for j in range(span_count)],
            out_specs=pl.BlockSpec((rows, heads * head), lambda r, *_: (r, 0)),
        ),
        compiler_params=pltpu.CompilerParams(vmem_limit_bytes=40 * 1024 * 1024),
        name="attend",
    )(senders, prefix_len, stretch_len, query, keys, values, *([incoming] * span_count))


def reduce_kernel(
    groups,
    pieces,
    rows_ref,
    weight_ref,
    out_ref,
    weight_buf,
    part,
    total,
    from_left,
    from_right,
    weight_sem,
    right_send,
    right_recv,
    left_send,
    left_recv,
):
    me = lax.axis_index("tp")
    wide = weight_buf.shape[3]
    last = groups - 1
    upper = jnp.where(me < groups // 2, 1, 0)

    def group_at(step):
        return upper * (last - step) + (1 - upper) * step

    def weight_copy(group, piece):
        start = pl.multiple_of((group * pieces + piece) * wide, wide)
        return pltpu.make_async_copy(
            weight_ref.at[:, pl.ds(start, wide)],
            weight_buf.at[group, piece],
            weight_sem.at[group, piece],
        )

    def right_copy(group, piece):
        return pltpu.make_async_remote_copy(
            src_ref=part.at[group, piece],
            dst_ref=from_left.at[group, piece],
            send_sem=right_send.at[group, piece],
            recv_sem=right_recv.at[group, piece],
            device_id={"tp": me + 1},
            device_id_type=pl.DeviceIdType.MESH,
        )

    def left_copy(group, piece):
        return pltpu.make_async_remote_copy(
            src_ref=part.at[group, piece],
            dst_ref=from_right.at[group, piece],
            send_sem=left_send.at[group, piece],
            recv_sem=left_recv.at[group, piece],
            device_id={"tp": me - 1},
            device_id_type=pl.DeviceIdType.MESH,
        )

    def each(body):
        def step(index, carry):
            body(index // pieces, index % pieces)
            return carry

        lax.fori_loop(0, groups * pieces, step, 0)

    each(lambda step, piece: weight_copy(group_at(step), piece).start())

    barrier = pltpu.get_barrier_semaphore()

    @pl.when(me > 0)
    def _():
        pl.semaphore_signal(
            barrier, inc=1, device_id={"tp": me - 1}, device_id_type=pl.DeviceIdType.MESH
        )

    @pl.when(me < last)
    def _():
        pl.semaphore_signal(
            barrier, inc=1, device_id={"tp": me + 1}, device_id_type=pl.DeviceIdType.MESH
        )

    pl.semaphore_wait(barrier, jnp.where(me > 0, 1, 0) + jnp.where(me < last, 1, 0))

    def produce(step, piece):
        group = group_at(step)
        weight_copy(group, piece).wait()
        product = jnp.dot(
            rows_ref[...], weight_buf[group, piece], preferred_element_type=jnp.float32
        ).astype(part.dtype)
        part[group, piece] = product

        @pl.when(group == me)
        def _():
            total[piece] = product.astype(jnp.float32)

        @pl.when((me == 0) & (group > me))
        def _():
            right_copy(group, piece).start()

        @pl.when((me == last) & (group < me))
        def _():
            left_copy(group, piece).start()

    each(produce)

    def add(group, piece, arrived):
        summed = part[group, piece].astype(jnp.float32) + arrived[group, piece].astype(jnp.float32)
        part[group, piece] = summed.astype(part.dtype)

    def pass_right(index):
        group, piece = last - index // pieces, index % pieces

        @pl.when(group >= me)
        def _():
            right_copy(group, piece).wait_recv()

        @pl.when(group > me)
        def _():
            add(group, piece, from_left)
            right_copy(group, piece).start()

        @pl.when(group == me)
        def _():
            total[piece] += from_left[group, piece].astype(jnp.float32)

    def pass_left(index):
        group, piece = index // pieces, index % pieces

        @pl.when(group <= me)
        def _():
            left_copy(group, piece).wait_recv()

        @pl.when(group < me)
        def _():
            add(group, piece, from_right)
            left_copy(group, piece).start()

        @pl.when(group == me)
        def _():
            total[piece] += from_right[group, piece].astype(jnp.float32)

    count = groups * pieces

    def pass_on(index, carry):
        right = index - (1 - upper)
        left = index - upper

        @pl.when((upper == 1) & (me > 0) & (right < count))
        def _():
            pass_right(right)

        @pl.when((me < last) & (left >= 0) & (left < count))
        def _():
            pass_left(left)

        @pl.when((upper == 0) & (me > 0) & (right >= 0))
        def _():
            pass_right(right)

        return carry

    lax.fori_loop(0, count + 1, pass_on, 0)

    for piece in range(pieces):
        out_ref[:, piece * wide : (piece + 1) * wide] = total[piece].astype(out_ref.dtype)

    def settle(group, piece):
        @pl.when(group > me)
        def _():
            right_copy(group, piece).wait_send()

        @pl.when(group < me)
        def _():
            left_copy(group, piece).wait_send()

    each(settle)


def projected_sum(rows, weight, groups):
    count, depth = rows.shape
    columns = weight.shape[1] // groups
    pieces = 4
    wide = columns // pieces
    slots = (groups, pieces, count, wide)
    return pl.pallas_call(
        functools.partial(reduce_kernel, groups, pieces),
        out_shape=jax.ShapeDtypeStruct((count, columns), jnp.bfloat16),
        in_specs=[
            pl.BlockSpec(memory_space=pltpu.VMEM),
            pl.BlockSpec(memory_space=pl.ANY),
        ],
        out_specs=pl.BlockSpec(memory_space=pltpu.VMEM),
        scratch_shapes=[
            pltpu.VMEM((groups, pieces, depth, wide), jnp.bfloat16),
            pltpu.VMEM(slots, jnp.bfloat16),
            pltpu.VMEM((pieces, count, wide), jnp.float32),
            pltpu.VMEM(slots, jnp.bfloat16),
            pltpu.VMEM(slots, jnp.bfloat16),
        ]
        + [pltpu.SemaphoreType.DMA((groups, pieces))] * 5,
        compiler_params=pltpu.CompilerParams(
            collective_id=0, has_side_effects=True, vmem_limit_bytes=44 * 1024 * 1024
        ),
        cost_estimate=pl.CostEstimate(
            flops=2 * count * depth * columns * groups,
            bytes_accessed=weight.size * 2,
            transcendentals=0,
        ),
        name="projected_sum",
    )(rows, weight)


def shards(
    stored_hidden,
    kv_weight,
    new_query,
    new_entries,
    out_weight,
    prefix_len,
    stretch_len,
    block_loc,
    owner,
):
    stores = lax.axis_size("store")
    own_store = lax.axis_index("store")
    local_blocks, block_rows, width = stored_hidden.shape
    request_count = owner.shape[0]
    per_owner = request_count // stores
    span_count = block_loc.shape[1]
    span = span_count * block_rows
    head = new_query.shape[2]
    query_heads = new_query.shape[1]
    kv_local = kv_weight.shape[2] // head
    group = query_heads // kv_local
    stretch = new_query.shape[0] // per_owner
    slot_ids = jnp.arange(request_count, dtype=jnp.int32)
    matched = owner[None, :] == slot_ids[:, None]
    request_of = jnp.sum(jnp.where(matched, slot_ids[None, :], 0), axis=1)
    locations = block_loc.reshape(-1)
    my_slots = own_store * per_owner + jnp.arange(per_owner, dtype=jnp.int32)
    my_requests = request_of[my_slots]
    senders = (block_loc[my_requests] // local_blocks).reshape(-1)
    local_ids = own_store * local_blocks + jnp.arange(local_blocks, dtype=jnp.int32)
    entry_ids = jnp.arange(locations.shape[0], dtype=jnp.int32)
    named = jnp.sum(
        jnp.where(locations[None, :] == local_ids[:, None], entry_ids[None, :], 0), axis=1
    )
    naming = (named // span_count)[:, None] == slot_ids[None, :]
    target = jnp.sum(jnp.where(naming, owner[None, :], 0), axis=1) // per_owner
    sent = project(
        target, named % span_count, stored_hidden, kv_weight, span_count, head, stores
    )
    incoming = lax.all_to_all(sent, "store", split_axis=0, concat_axis=0, tiled=True)
    attended = attend(
        senders,
        prefix_len[my_requests],
        stretch_len[my_requests],
        jnp.transpose(new_query, (1, 0, 2)),
        jnp.transpose(new_entries[:, 0], (1, 0, 2)),
        jnp.transpose(new_entries[:, 1], (1, 0, 2)),
        incoming,
    )
    return projected_sum(attended, out_weight, lax.axis_size("tp"))


def solution(mesh):
    in_specs = (
        P("store", None, None),
        P(None, None, "tp"),
        P("store", "tp", None),
        P("store", None, "tp", None),
        P("tp", None),
        P(),
        P(),
        P(),
        P(),
    )
    out_specs = P("store", "tp")
    return jax.shard_map(shards, mesh=mesh, in_specs=in_specs, out_specs=out_specs, check_vma=False)
```

```python
import functools

import jax
import jax.numpy as jnp
import numpy as np
from jax import lax
from jax.experimental import pallas as pl
from jax.experimental.pallas import tpu as pltpu
from jax.sharding import PartitionSpec as P

rope_base = 500000.0
mask_fill = -1e30


def rotary_table(span, head):
    half = head // 2
    exponents = -(np.arange(half, dtype=np.float32) * np.float32(2.0 / head))
    inverse = np.power(np.float32(rope_base), exponents)
    angles = np.arange(span, dtype=np.float32)[:, None] * inverse[None, :]
    cosine = np.cos(angles)
    sine = np.sin(angles)
    return (
        np.concatenate([cosine, cosine], axis=1),
        np.concatenate([-sine, sine], axis=1),
    )


def project_kernel(
    target_ref, place_ref, hidden_ref, weight_ref, cosine_ref, sine_ref, out_ref, sums
):
    step = pl.program_id(0)
    head = cosine_ref.shape[2]
    wide = weight_ref.shape[2]
    blocks, block_rows, depth = hidden_ref.shape
    hidden = hidden_ref[...].reshape(blocks * block_rows, depth)
    parts = jnp.swapaxes(weight_ref[...], 0, 1)
    both = jnp.concatenate([parts[0], parts[1]], axis=1)

    @pl.when(step == 0)
    def _():
        sums[...] = jnp.zeros_like(sums)

    sums[...] += jnp.dot(hidden, both, preferred_element_type=jnp.float32)

    @pl.when(step == pl.num_programs(0) - 1)
    def _():
        for block in range(blocks):
            rows = pl.ds(block * block_rows, block_rows)
            cosine = cosine_ref[place_ref[block]]
            sine = sine_ref[place_ref[block]]
            slot = target_ref[block]
            for start in range(0, wide, head):
                part = sums[rows, start : start + head]
                turned = part * cosine + pltpu.roll(part, head // 2, 1) * sine
                out_ref[slot, :, start : start + head] = turned.astype(out_ref.dtype)
            out_ref[slot, :, wide:] = sums[rows, wide:].astype(out_ref.dtype)


def project(target, place, hidden, weight, span_count, head, slots, kv):
    blocks, block_rows, width = hidden.shape
    wide = head
    depth = 2048
    cosine, sine = rotary_table(span_count * block_rows, head)
    table = (span_count, block_rows, head)
    whole = lambda shape: pl.BlockSpec(shape, lambda step, *_: (0,) * len(shape))
    return pl.pallas_call(
        project_kernel,
        out_shape=jax.ShapeDtypeStruct((slots, block_rows, 2 * wide), jnp.bfloat16),
        grid_spec=pltpu.PrefetchScalarGridSpec(
            num_scalar_prefetch=2,
            grid=(width // depth,),
            in_specs=[
                pl.BlockSpec((blocks, block_rows, depth), lambda step, *_: (0, 0, step)),
                pl.BlockSpec((depth, 2, wide), lambda step, *_: (step, 0, kv)),
                whole(table),
                whole(table),
            ],
            out_specs=whole((slots, block_rows, 2 * wide)),
            scratch_shapes=[pltpu.VMEM((blocks * block_rows, 2 * wide), jnp.float32)],
        ),
        compiler_params=pltpu.CompilerParams(vmem_limit_bytes=60 * 1024 * 1024),
        cost_estimate=pl.CostEstimate(
            flops=4 * hidden.size * wide, bytes_accessed=2 * hidden.size, transcendentals=0
        ),
        name="project",
    )(target, place, hidden, weight, cosine.reshape(table), sine.reshape(table))


def attend_kernel(
    sender_ref, prefix_ref, stretch_ref, query_ref, key_ref, value_ref, *block_refs_and_out
):
    block_refs, out_ref = block_refs_and_out[:-1], block_refs_and_out[-1]
    request = pl.program_id(0)
    heads, rows, head = query_ref.shape
    kv_heads = key_ref.shape[0]
    group = heads // kv_heads
    span_count = len(block_refs) // kv_heads
    span = span_count * block_refs[0].shape[1]
    scale = head ** (-0.5)
    prefix_live = lax.broadcasted_iota(jnp.int32, (rows, span), 1) < prefix_ref[request]
    row_ids = lax.broadcasted_iota(jnp.int32, (rows, rows), 0)
    causal = lax.broadcasted_iota(jnp.int32, (rows, rows), 1) <= row_ids
    live = lax.broadcasted_iota(jnp.int32, (rows, head), 0) < stretch_ref[request]
    contract_last = (((1,), (1,)), ((), ()))
    for kv in range(kv_heads):
        own_refs = block_refs[kv * span_count : (kv + 1) * span_count]
        keys = jnp.concatenate([ref[0, :, :head] for ref in own_refs], axis=0)
        values = jnp.concatenate([ref[0, :, head:] for ref in own_refs], axis=0)
        new_keys = key_ref[kv]
        new_values = value_ref[kv]
        for index in range(group):
            h = kv * group + index
            query = query_ref[h]
            early = lax.dot_general(
                query, keys, contract_last, preferred_element_type=jnp.float32
            )
            recent = lax.dot_general(
                query, new_keys, contract_last, preferred_element_type=jnp.float32
            )
            early = jnp.where(prefix_live, early * scale, mask_fill)
            recent = jnp.where(causal, recent * scale, mask_fill)
            top = jnp.maximum(
                jnp.max(early, axis=1, keepdims=True), jnp.max(recent, axis=1, keepdims=True)
            )
            early_w = jnp.exp(early - top)
            recent_w = jnp.exp(recent - top)
            total = jnp.sum(early_w, axis=1, keepdims=True) + jnp.sum(
                recent_w, axis=1, keepdims=True
            )
            attended = jnp.dot(
                early_w.astype(jnp.bfloat16), values, preferred_element_type=jnp.float32
            ) + jnp.dot(
                recent_w.astype(jnp.bfloat16), new_values, preferred_element_type=jnp.float32
            )
            attended = jnp.where(live, attended / total, 0.0)
            out_ref[:, h * head : (h + 1) * head] = attended.astype(out_ref.dtype)


def attend(senders, prefix_len, stretch_len, query, keys, values, incoming):
    heads, count, head = query.shape
    kv_heads = keys.shape[0]
    requests = prefix_len.shape[0]
    rows = count // requests
    span_count = senders.shape[0] // requests
    _, block_rows, wide = incoming[0].shape

    def block_spec(j):
        return pl.BlockSpec(
            (1, block_rows, wide), lambda r, sender, *_: (sender[r * span_count + j], 0, 0)
        )

    return pl.pallas_call(
        attend_kernel,
        out_shape=jax.ShapeDtypeStruct((count, heads * head), jnp.bfloat16),
        grid_spec=pltpu.PrefetchScalarGridSpec(
            num_scalar_prefetch=3,
            grid=(requests,),
            in_specs=[
                pl.BlockSpec((heads, rows, head), lambda r, *_: (0, r, 0)),
                pl.BlockSpec((kv_heads, rows, head), lambda r, *_: (0, r, 0)),
                pl.BlockSpec((kv_heads, rows, head), lambda r, *_: (0, r, 0)),
            ]
            + [block_spec(j) for j in range(span_count)] * kv_heads,
            out_specs=pl.BlockSpec((rows, heads * head), lambda r, *_: (r, 0)),
        ),
        compiler_params=pltpu.CompilerParams(vmem_limit_bytes=40 * 1024 * 1024),
        name="attend",
    )(senders, prefix_len, stretch_len, query, keys, values, *[blocks for blocks in incoming for _ in range(span_count)])


def reduce_kernel(
    groups,
    pieces,
    rows_ref,
    weight_ref,
    out_ref,
    weight_buf,
    part,
    total,
    from_left,
    from_right,
    weight_sem,
    right_send,
    right_recv,
    left_send,
    left_recv,
):
    me = lax.axis_index("tp")
    wide = weight_buf.shape[3]
    last = groups - 1
    upper = jnp.where(me < groups // 2, 1, 0)

    def group_at(step):
        return upper * (last - step) + (1 - upper) * step

    def weight_copy(group, piece):
        start = pl.multiple_of((group * pieces + piece) * wide, wide)
        return pltpu.make_async_copy(
            weight_ref.at[:, pl.ds(start, wide)],
            weight_buf.at[group, piece],
            weight_sem.at[group, piece],
        )

    def right_copy(group, piece):
        return pltpu.make_async_remote_copy(
            src_ref=part.at[group, piece],
            dst_ref=from_left.at[group, piece],
            send_sem=right_send.at[group, piece],
            recv_sem=right_recv.at[group, piece],
            device_id={"tp": me + 1},
            device_id_type=pl.DeviceIdType.MESH,
        )

    def left_copy(group, piece):
        return pltpu.make_async_remote_copy(
            src_ref=part.at[group, piece],
            dst_ref=from_right.at[group, piece],
            send_sem=left_send.at[group, piece],
            recv_sem=left_recv.at[group, piece],
            device_id={"tp": me - 1},
            device_id_type=pl.DeviceIdType.MESH,
        )

    def each(body):
        def step(index, carry):
            body(index // pieces, index % pieces)
            return carry

        lax.fori_loop(0, groups * pieces, step, 0)

    each(lambda step, piece: weight_copy(group_at(step), piece).start())

    barrier = pltpu.get_barrier_semaphore()

    @pl.when(me > 0)
    def _():
        pl.semaphore_signal(
            barrier, inc=1, device_id={"tp": me - 1}, device_id_type=pl.DeviceIdType.MESH
        )

    @pl.when(me < last)
    def _():
        pl.semaphore_signal(
            barrier, inc=1, device_id={"tp": me + 1}, device_id_type=pl.DeviceIdType.MESH
        )

    pl.semaphore_wait(barrier, jnp.where(me > 0, 1, 0) + jnp.where(me < last, 1, 0))

    def produce(step, piece):
        group = group_at(step)
        weight_copy(group, piece).wait()
        product = jnp.dot(
            rows_ref[...], weight_buf[group, piece], preferred_element_type=jnp.float32
        ).astype(part.dtype)
        part[group, piece] = product

        @pl.when(group == me)
        def _():
            total[piece] = product.astype(jnp.float32)

        @pl.when((me == 0) & (group > me))
        def _():
            right_copy(group, piece).start()

        @pl.when((me == last) & (group < me))
        def _():
            left_copy(group, piece).start()

    each(produce)

    def add(group, piece, arrived):
        summed = part[group, piece].astype(jnp.float32) + arrived[group, piece].astype(jnp.float32)
        part[group, piece] = summed.astype(part.dtype)

    def pass_right(index):
        group, piece = last - index // pieces, index % pieces

        @pl.when(group >= me)
        def _():
            right_copy(group, piece).wait_recv()

        @pl.when(group > me)
        def _():
            add(group, piece, from_left)
            right_copy(group, piece).start()

        @pl.when(group == me)
        def _():
            total[piece] += from_left[group, piece].astype(jnp.float32)

    def pass_left(index):
        group, piece = index // pieces, index % pieces

        @pl.when(group <= me)
        def _():
            left_copy(group, piece).wait_recv()

        @pl.when(group < me)
        def _():
            add(group, piece, from_right)
            left_copy(group, piece).start()

        @pl.when(group == me)
        def _():
            total[piece] += from_right[group, piece].astype(jnp.float32)

    count = groups * pieces

    def pass_on(index, carry):
        right = index - (1 - upper)
        left = index - upper

        @pl.when((upper == 1) & (me > 0) & (right < count))
        def _():
            pass_right(right)

        @pl.when((me < last) & (left >= 0) & (left < count))
        def _():
            pass_left(left)

        @pl.when((upper == 0) & (me > 0) & (right >= 0))
        def _():
            pass_right(right)

        return carry

    lax.fori_loop(0, count + 1, pass_on, 0)

    for piece in range(pieces):
        out_ref[:, piece * wide : (piece + 1) * wide] = total[piece].astype(out_ref.dtype)

    def settle(group, piece):
        @pl.when(group > me)
        def _():
            right_copy(group, piece).wait_send()

        @pl.when(group < me)
        def _():
            left_copy(group, piece).wait_send()

    each(settle)


def projected_sum(rows, weight, groups):
    count, depth = rows.shape
    columns = weight.shape[1] // groups
    pieces = 4
    wide = columns // pieces
    slots = (groups, pieces, count, wide)
    return pl.pallas_call(
        functools.partial(reduce_kernel, groups, pieces),
        out_shape=jax.ShapeDtypeStruct((count, columns), jnp.bfloat16),
        in_specs=[
            pl.BlockSpec(memory_space=pltpu.VMEM),
            pl.BlockSpec(memory_space=pl.ANY),
        ],
        out_specs=pl.BlockSpec(memory_space=pltpu.VMEM),
        scratch_shapes=[
            pltpu.VMEM((groups, pieces, depth, wide), jnp.bfloat16),
            pltpu.VMEM(slots, jnp.bfloat16),
            pltpu.VMEM((pieces, count, wide), jnp.float32),
            pltpu.VMEM(slots, jnp.bfloat16),
            pltpu.VMEM(slots, jnp.bfloat16),
        ]
        + [pltpu.SemaphoreType.DMA((groups, pieces))] * 5,
        compiler_params=pltpu.CompilerParams(
            collective_id=0, has_side_effects=True, vmem_limit_bytes=44 * 1024 * 1024
        ),
        cost_estimate=pl.CostEstimate(
            flops=2 * count * depth * columns * groups,
            bytes_accessed=weight.size * 2,
            transcendentals=0,
        ),
        name="projected_sum",
    )(rows, weight)


def shards(
    stored_hidden,
    kv_weight,
    new_query,
    new_entries,
    out_weight,
    prefix_len,
    stretch_len,
    block_loc,
    owner,
):
    stores = lax.axis_size("store")
    own_store = lax.axis_index("store")
    local_blocks, block_rows, width = stored_hidden.shape
    request_count = owner.shape[0]
    per_owner = request_count // stores
    span_count = block_loc.shape[1]
    span = span_count * block_rows
    head = new_query.shape[2]
    query_heads = new_query.shape[1]
    kv_local = kv_weight.shape[2] // head
    group = query_heads // kv_local
    stretch = new_query.shape[0] // per_owner
    slot_ids = jnp.arange(request_count, dtype=jnp.int32)
    matched = owner[None, :] == slot_ids[:, None]
    request_of = jnp.sum(jnp.where(matched, slot_ids[None, :], 0), axis=1)
    locations = block_loc.reshape(-1)
    my_slots = own_store * per_owner + jnp.arange(per_owner, dtype=jnp.int32)
    my_requests = request_of[my_slots]
    senders = (block_loc[my_requests] // local_blocks).reshape(-1)
    local_ids = own_store * local_blocks + jnp.arange(local_blocks, dtype=jnp.int32)
    entry_ids = jnp.arange(locations.shape[0], dtype=jnp.int32)
    named = jnp.sum(
        jnp.where(locations[None, :] == local_ids[:, None], entry_ids[None, :], 0), axis=1
    )
    naming = (named // span_count)[:, None] == slot_ids[None, :]
    target = jnp.sum(jnp.where(naming, owner[None, :], 0), axis=1) // per_owner
    incoming = []
    for kv in range(kv_local):
        sent = project(
            target, named % span_count, stored_hidden, kv_weight, span_count, head, stores, kv
        )
        incoming.append(lax.all_to_all(sent, "store", split_axis=0, concat_axis=0, tiled=True))
    attended = attend(
        senders,
        prefix_len[my_requests],
        stretch_len[my_requests],
        jnp.transpose(new_query, (1, 0, 2)),
        jnp.transpose(new_entries[:, 0], (1, 0, 2)),
        jnp.transpose(new_entries[:, 1], (1, 0, 2)),
        incoming,
    )
    return projected_sum(attended, out_weight, lax.axis_size("tp"))


def solution(mesh):
    in_specs = (
        P("store", None, None),
        P(None, None, "tp"),
        P("store", "tp", None),
        P("store", None, "tp", None),
        P("tp", None),
        P(),
        P(),
        P(),
        P(),
    )
    out_specs = P("store", "tp")
    return jax.shard_map(shards, mesh=mesh, in_specs=in_specs, out_specs=out_specs, check_vma=False)
```
